32 devices in a mesh: groups: 2 (over y), img: 4 (over z), cap: 4 (over x, core).
Axes of the slice: x: 2, y: 2, z: 4, core: 2. Of those that a mesh axis runs over, the one named last changes fastest.
Arguments:
- text_states: bfloat16 [512, 32, 768], P(('groups', 'img', 'cap')), parts along dimension 0, may hold values from -170 to 170
- text_lens: int32 [512], P(('groups', 'img', 'cap')), parts along dimension 0, may hold values from 8 to 32
- text_proj: bfloat16 [768, 256], replicated, may hold values from -1.75 to 1.75
- query_states: bfloat16 [192, 32, 768], P(('groups', 'img')), parts along dimension 0, may hold values from -170 to 170
- vision_proj: bfloat16 [768, 256], replicated, may hold values from -1.75 to 1.75
- student_text: bfloat16 [512, 512], P(('groups', 'img', 'cap')), parts along dimension 0, may hold values from -6 to 6
- student_feats: bfloat16 [192, 768], P(('groups', 'img')), parts along dimension 0, may hold values from -170 to 170
- student_proj: bfloat16 [768, 512], replicated, may hold values from -1.75 to 1.75
- candidates: int32 [512, 64], P(('groups', 'img', 'cap')), parts along dimension 0, may hold values from 0 to 95, as said below
Outputs:
- losses: float32 [512], P(('groups', 'img', 'cap')), parts along dimension 0
- proj_grad: float32 [1536, 512], P('groups'), parts along dimension 0
The draws below stay inside these ranges and needn't reach their ends.
There are 2 independent parts, one for each index of `groups`. The reference program is written for one: setup_inputs(seed, part) draws one part's arguments, and reference() takes and returns one part's arrays. A program takes and returns all parts, laid end to end along the dimension named above; an argument that names none is the same for every part. Nothing has to cross between parts.
Inputs may be any that keep to these rules, and one draw needn't show every extreme that they name: Each row of candidates is 8 blocks of 8 consecutive entries; the ids of one block are distinct and all belong to one index of img (id // 24). The blocks of the 16 captions of one device name one index of img at most 64 times, and exactly 64 times for some index.
All inputs are finite; a program needn't handle non-finite values.
Results may differ from the reference program's by a relative error of at most 0.004.
Values may be sent and summed in bfloat16 or wider, within the bound.
A program may use at most 64 MiB of HBM per device.

```python
import jax
import jax.numpy as jnp
from jax import lax

TXT = 768
ITC = 256
NQ = 32
LEN = 32
SW = 768
SE = 512
CAND = 64
BLOCK = 8
IMG_DEV = 24
CAP_DEV = 16
SLOT = 64
CAPS = 256
IMAGES = 96
N_IMG = 4
N_CAP = 4


def drawn_normal(key, array_shape, limit_value):
    return jnp.clip(jax.random.normal(key, array_shape, jnp.float32), -limit_value, limit_value)


def scaled_weight(key, row_count, column_count):
    return drawn_normal(key, (row_count, column_count), 6.0) * row_count ** (-0.5)


def draw_text_states(key, part):
    key = jax.random.fold_in(key, 21)
    values = drawn_normal(key, (CAPS, LEN, TXT), 6.0)
    return values.astype(jnp.bfloat16)


def draw_query_states(key, part):
    key = jax.random.fold_in(key, 23)
    values = drawn_normal(key, (IMAGES, NQ, TXT), 6.0)
    return values.astype(jnp.bfloat16)


def draw_text_proj(key, part):
    key = jax.random.fold_in(key, 25)
    values = scaled_weight(key, TXT, ITC)
    return values.astype(jnp.bfloat16)


def draw_vision_proj(key, part):
    key = jax.random.fold_in(key, 27)
    values = scaled_weight(key, TXT, ITC)
    return values.astype(jnp.bfloat16)


def draw_student_text(key, part):
    key = jax.random.fold_in(key, 31)
    values = drawn_normal(key, (CAPS, SE), 6.0)
    return values.astype(jnp.bfloat16)


def draw_student_feats(key, part):
    key = jax.random.fold_in(key, 33)
    values = drawn_normal(key, (IMAGES, SW), 6.0)
    return values.astype(jnp.bfloat16)


def draw_student_proj(key, part):
    key = jax.random.fold_in(key, 35)
    values = scaled_weight(key, SW, SE)
    return values.astype(jnp.bfloat16)


def draw_candidates(key, part):
    key = jax.random.fold_in(key, 11)
    block_total = CAP_DEV * (CAND // BLOCK)
    pool_size = N_IMG * SLOT
    owner_pool = jnp.repeat(jnp.arange(N_IMG, dtype=jnp.int32), SLOT)

    def pick_block(block_key):
        return jax.random.permutation(block_key, IMG_DEV)[:BLOCK].astype(jnp.int32)

    def one_device(device):
        device_key = jax.random.fold_in(key, device)
        hot_key, order_key, shuffle_key, local_key = jax.random.split(device_key, 4)
        hottest = jax.random.randint(hot_key, (), 0, N_IMG)
        noise_draw = jax.random.randint(order_key, (pool_size,), 0, 65536)
        ranking = (noise_draw + 65536 * (owner_pool == hottest).astype(jnp.int32)) * pool_size + jnp.arange(pool_size, dtype=jnp.int32)
        ordering = jnp.argsort(-ranking)
        owners = owner_pool[ordering[:block_total]]
        owners = jax.random.permutation(shuffle_key, owners)
        local_ids = jax.vmap(pick_block)(jax.random.split(local_key, block_total))
        return (owners[:, None] * IMG_DEV + local_ids).reshape(CAP_DEV, CAND)
    devices = jnp.arange(N_IMG * N_CAP, dtype=jnp.int32)
    return jax.vmap(one_device)(devices).reshape(CAP_DEV * N_IMG * N_CAP, CAND).astype(jnp.int32)


def plant(entries, key, smallest, high):
    longest = entries.shape.index(max(entries.shape))
    spots = []
    for shift in (0, 1):
        where = [jax.random.randint(jax.random.fold_in(key, axis), (), 0, length) for axis, length in enumerate(entries.shape)]
        where[longest] = (where[longest] + shift) % entries.shape[longest]
        spots.append(tuple(where))
    return entries.at[spots[0]].set(smallest).at[spots[1]].set(high)


def setup_inputs(seed: int = 0, part: int = 0) -> dict:
    key_of = jax.random.split(jax.random.key(seed), 10)
    own_keys = jax.random.split(jax.random.fold_in(key_of[9], part), 10)
    text_states = draw_text_states(jax.random.fold_in(jax.random.fold_in(key_of[9], part), 71), part)
    text_lens = plant(jax.random.randint(own_keys[1], (CAPS,), LEN // 4, LEN + 1), jax.random.fold_in(own_keys[1], 1), LEN // 4, LEN).astype(jnp.int32)
    text_proj = draw_text_proj(jax.random.fold_in(key_of[9], 71), part)
    query_states = draw_query_states(jax.random.fold_in(jax.random.fold_in(key_of[9], part), 71), part)
    vision_proj = draw_vision_proj(jax.random.fold_in(key_of[9], 71), part)
    student_text = draw_student_text(jax.random.fold_in(jax.random.fold_in(key_of[9], part), 71), part)
    student_feats = draw_student_feats(jax.random.fold_in(jax.random.fold_in(key_of[9], part), 71), part)
    student_proj = draw_student_proj(jax.random.fold_in(key_of[9], 71), part)
    candidates = draw_candidates(jax.random.fold_in(jax.random.fold_in(key_of[9], part), 71), part)
    return {"text_states": text_states, "text_lens": text_lens, "text_proj": text_proj, "query_states": query_states, "vision_proj": vision_proj, "student_text": student_text, "student_feats": student_feats, "student_proj": student_proj, "candidates": candidates}


TEACHER_TEMP = 0.01
LOGIT_SCALE = 100.0

def unit_rows(values):
    return values * lax.rsqrt(lax.optimization_barrier(jnp.sum(values * values, axis=-1, keepdims=True)) + 1e-06)

def reference(text_states, text_lens, text_proj, query_states, vision_proj, student_text, student_feats, student_proj, candidates):
    token_rows = unit_rows(jnp.einsum('clw,wd->cld', text_states.astype(jnp.float32), text_proj.astype(jnp.float32))).astype(jnp.bfloat16)
    query_rows = unit_rows(jnp.einsum('iqw,wd->iqd', query_states.astype(jnp.float32), vision_proj.astype(jnp.float32))).astype(jnp.bfloat16)
    image_embed = jnp.dot(student_feats, student_proj, preferred_element_type=jnp.float32)
    image_norm = jnp.sqrt(lax.optimization_barrier(jnp.sum(image_embed * image_embed, axis=-1)) + 1e-06)
    image_unit = image_embed / image_norm[:, None]
    text_unit = unit_rows(student_text.astype(jnp.float32))
    group_count = CAPS // CAP_DEV
    grouped_tokens = token_rows.reshape(group_count, CAP_DEV, LEN, ITC)
    grouped_lens = text_lens.reshape(group_count, CAP_DEV)
    grouped_ids = candidates.reshape(group_count, CAP_DEV, CAND)
    grouped_text = text_unit.reshape(group_count, CAP_DEV, SE)

    def score_group(inputs):
        tok_group, len_group, id_group, unit_group = inputs
        picked = query_rows[id_group].astype(jnp.float32)
        products = jnp.einsum('clt,ckqt->cklq', tok_group.astype(jnp.float32), picked)
        strongest = lax.optimization_barrier(jnp.max(products, axis=-1))
        valid_mask = jnp.arange(LEN)[None, :] < len_group[:, None]
        summed = lax.optimization_barrier(jnp.sum(jnp.where(valid_mask[:, None, :], strongest, 0.0), axis=-1))
        teacher_group = summed / len_group[:, None].astype(jnp.float32) / TEACHER_TEMP
        cosine = lax.optimization_barrier(jnp.sum(unit_group[:, None, :] * image_unit[id_group], axis=-1))
        return (teacher_group, LOGIT_SCALE * cosine)
    teacher, student = lax.map(score_group, (grouped_tokens, grouped_lens, grouped_ids, grouped_text))
    teacher = teacher.reshape(CAPS, CAND)
    student = student.reshape(CAPS, CAND)
    teacher_log = jax.nn.log_softmax(teacher, axis=-1)
    student_log = jax.nn.log_softmax(student, axis=-1)
    teacher_prob = jnp.exp(teacher_log)
    losses = lax.optimization_barrier(jnp.sum(teacher_prob * (teacher_log - student_log), axis=-1))
    score_grad = jnp.exp(student_log) - teacher_prob

    def add_group(running, inputs):
        grad_group, id_group, unit_group = inputs
        scaled = LOGIT_SCALE * grad_group
        picked_unit = image_unit[id_group]
        cosine = lax.optimization_barrier(jnp.sum(unit_group[:, None, :] * picked_unit, axis=-1))
        pair_terms = scaled[..., None] * (unit_group[:, None, :] - cosine[..., None] * picked_unit) / image_norm[id_group][..., None]
        return (running.at[id_group.reshape(-1)].add(pair_terms.reshape(-1, SE)), None)
    embed_grad = lax.scan(add_group, jnp.zeros((IMAGES, SE), jnp.float32), (score_grad.reshape(group_count, CAP_DEV, CAND), grouped_ids, grouped_text))[0]
    proj_grad = jnp.dot(student_feats.astype(jnp.float32).T, embed_grad, precision=lax.Precision.HIGHEST)
    return (losses, proj_grad)
```

```python
import jax
import jax.numpy as jnp
from jax import lax
from jax.sharding import PartitionSpec as P

TEACHER_TEMP = 0.01
LOGIT_SCALE = 100.0
HIGHEST = lax.Precision.HIGHEST


def unit_rows(values):
    return values * lax.rsqrt(jnp.sum(values * values, axis=-1, keepdims=True) + 1e-06)


def local(
    text_states,
    text_lens,
    text_proj,
    query_states,
    vision_proj,
    student_text,
    student_feats,
    student_proj,
    candidates,
):
    cap_dev, length, txt_width = text_states.shape
    img_dev = query_states.shape[0]
    query_rows = unit_rows(
        jnp.dot(
            query_states.reshape(-1, txt_width), vision_proj, preferred_element_type=jnp.float32
        )
    ).astype(jnp.bfloat16)
    all_rows = lax.all_gather(query_rows, "img", axis=0, tiled=False)
    all_feats = lax.all_gather(student_feats, "img", axis=0, tiled=True)
    all_text = lax.all_gather(student_text, ("img", "cap"), axis=0, tiled=True)
    token_rows = unit_rows(
        jnp.dot(text_states.reshape(-1, txt_width), text_proj, preferred_element_type=jnp.float32)
    ).astype(jnp.bfloat16)
    img_count = lax.axis_size("img")
    images = img_count * img_dev

    valid_mask = jnp.arange(length)[None, :] < text_lens[:, None]
    pieces = []
    for owner in range(img_count):
        products = jnp.dot(
            token_rows, all_rows[owner].T, preferred_element_type=jnp.float32
        ).reshape(cap_dev, length, img_dev, -1)
        strongest = jnp.max(products, axis=-1)
        pieces.append(jnp.sum(jnp.where(valid_mask[:, :, None], strongest, 0.0), axis=1))
    summed = jnp.concatenate(pieces, axis=1)
    teacher = summed / text_lens[:, None].astype(jnp.float32) / TEACHER_TEMP

    image_embed = jnp.dot(all_feats, student_proj, preferred_element_type=jnp.float32)
    image_norm = jnp.sqrt(jnp.sum(image_embed * image_embed, axis=-1) + 1e-06)
    image_unit = image_embed / image_norm[:, None]
    text_unit = unit_rows(student_text.astype(jnp.float32))
    cosine = jnp.dot(text_unit, image_unit.T, precision=HIGHEST)
    student = LOGIT_SCALE * cosine

    counts = jnp.sum(
        (candidates[:, :, None] == jnp.arange(images)[None, None, :]).astype(jnp.float32), axis=1
    )
    present = counts > 0

    def log_softmax(scores):
        peak = jnp.max(jnp.where(present, scores, -jnp.inf), axis=1, keepdims=True)
        shifted = jnp.where(present, scores - peak, 0.0)
        total = jnp.sum(counts * jnp.exp(shifted), axis=1, keepdims=True)
        return shifted - jnp.log(total)

    teacher_log = log_softmax(teacher)
    student_log = log_softmax(student)
    teacher_prob = jnp.exp(teacher_log)
    losses = jnp.sum(counts * teacher_prob * (teacher_log - student_log), axis=1)
    spread = LOGIT_SCALE * counts * (jnp.exp(student_log) - teacher_prob)
    radial = jnp.sum(spread * cosine, axis=0, keepdims=True)
    all_spread = lax.all_gather(
        jnp.concatenate([spread, radial], axis=0), ("img", "cap"), axis=0, tiled=False
    )
    radial = jnp.sum(all_spread[:, cap_dev], axis=0)
    all_spread = all_spread[:, :cap_dev].reshape(-1, images)
    all_unit = unit_rows(all_text.astype(jnp.float32))
    embed_grad = (
        jnp.einsum("ci,cd->id", all_spread, all_unit, precision=HIGHEST)
        - radial[:, None] * image_unit
    ) / image_norm[:, None]
    top = lax.optimization_barrier(embed_grad.astype(jnp.bfloat16))
    rest = (embed_grad - top.astype(jnp.float32)).astype(jnp.bfloat16)
    proj_grad = jnp.einsum(
        "is,id->sd",
        jnp.concatenate([all_feats, all_feats], axis=0),
        jnp.concatenate([top, rest], axis=0),
        preferred_element_type=jnp.float32,
    )
    return (losses, proj_grad)


def solution(mesh):
    in_specs = (
        P(("groups", "img", "cap"), None, None),
        P(("groups", "img", "cap")),
        P(),
        P(("groups", "img"), None, None),
        P(),
        P(("groups", "img", "cap"), None),
        P(("groups", "img"), None),
        P(),
        P(("groups", "img", "cap"), None),
    )
    out_specs = (P(("groups", "img", "cap")), P("groups", None))
    return jax.shard_map(local, mesh=mesh, in_specs=in_specs, out_specs=out_specs, check_vma=False)
```

```python
import jax
import jax.numpy as jnp
from jax import lax
from jax.experimental import pallas as pl
from jax.experimental.pallas import tpu as pltpu
from jax.sharding import PartitionSpec as P

TEACHER_TEMP = 0.01
LOGIT_SCALE = 100.0
HIGHEST = lax.Precision.HIGHEST


def unit_rows(values):
    return values * lax.rsqrt(jnp.sum(values * values, axis=-1, keepdims=True) + 1e-06)


def gathered(
    text_states,
    text_lens,
    text_proj,
    query_states,
    vision_proj,
    student_text,
    student_feats,
    student_proj,
    candidates,
):
    cap_dev, length, txt_width = text_states.shape
    img_dev = query_states.shape[0]
    query_rows = unit_rows(
        jnp.dot(
            query_states.reshape(-1, txt_width), vision_proj, preferred_element_type=jnp.float32
        )
    ).astype(jnp.bfloat16)
    all_rows = lax.all_gather(query_rows, "img", axis=0, tiled=False)
    all_feats = lax.all_gather(student_feats, "img", axis=0, tiled=True)
    all_text = lax.all_gather(student_text, ("img", "cap"), axis=0, tiled=True)
    token_rows = unit_rows(
        jnp.dot(text_states.reshape(-1, txt_width), text_proj, preferred_element_type=jnp.float32)
    ).astype(jnp.bfloat16)
    img_count = lax.axis_size("img")
    images = img_count * img_dev

    valid_mask = jnp.arange(length)[None, :] < text_lens[:, None]
    pieces = []
    for owner in range(img_count):
        products = jnp.dot(
            token_rows, all_rows[owner].T, preferred_element_type=jnp.float32
        ).reshape(cap_dev, length, img_dev, -1)
        strongest = jnp.max(products, axis=-1)
        pieces.append(jnp.sum(jnp.where(valid_mask[:, :, None], strongest, 0.0), axis=1))
    summed = jnp.concatenate(pieces, axis=1)
    teacher = summed / text_lens[:, None].astype(jnp.float32) / TEACHER_TEMP

    image_embed = jnp.dot(all_feats, student_proj, preferred_element_type=jnp.float32)
    image_norm = jnp.sqrt(jnp.sum(image_embed * image_embed, axis=-1) + 1e-06)
    image_unit = image_embed / image_norm[:, None]
    text_unit = unit_rows(student_text.astype(jnp.float32))
    cosine = jnp.dot(text_unit, image_unit.T, precision=HIGHEST)
    student = LOGIT_SCALE * cosine

    counts = jnp.sum(
        (candidates[:, :, None] == jnp.arange(images)[None, None, :]).astype(jnp.float32), axis=1
    )
    present = counts > 0

    def log_softmax(scores):
        peak = jnp.max(jnp.where(present, scores, -jnp.inf), axis=1, keepdims=True)
        shifted = jnp.where(present, scores - peak, 0.0)
        total = jnp.sum(counts * jnp.exp(shifted), axis=1, keepdims=True)
        return shifted - jnp.log(total)

    teacher_log = log_softmax(teacher)
    student_log = log_softmax(student)
    teacher_prob = jnp.exp(teacher_log)
    losses = jnp.sum(counts * teacher_prob * (teacher_log - student_log), axis=1)
    spread = LOGIT_SCALE * counts * (jnp.exp(student_log) - teacher_prob)
    radial = jnp.sum(spread * cosine, axis=0, keepdims=True)
    all_spread = lax.all_gather(
        jnp.concatenate([spread, radial], axis=0), ("img", "cap"), axis=0, tiled=False
    )
    radial = jnp.sum(all_spread[:, cap_dev], axis=0)
    all_spread = all_spread[:, :cap_dev].reshape(-1, images)
    all_unit = unit_rows(all_text.astype(jnp.float32))
    embed_grad = (
        jnp.einsum("ci,cd->id", all_spread, all_unit, precision=HIGHEST)
        - radial[:, None] * image_unit
    ) / image_norm[:, None]
    top = lax.optimization_barrier(embed_grad.astype(jnp.bfloat16))
    rest = (embed_grad - top.astype(jnp.float32)).astype(jnp.bfloat16)
    proj_grad = jnp.einsum(
        "is,id->sd",
        jnp.concatenate([all_feats, all_feats], axis=0),
        jnp.concatenate([top, rest], axis=0),
        preferred_element_type=jnp.float32,
    )
    return (losses, proj_grad)


MESH = pl.DeviceIdType.MESH
LAST = (((1,), (1,)), ((), ()))
NEAR_FIRST = (1, 3, 2)


def split_three(values):
    top = values.astype(jnp.bfloat16)
    rest = values - top.astype(jnp.float32)
    middle = rest.astype(jnp.bfloat16)
    low = (rest - middle.astype(jnp.float32)).astype(jnp.bfloat16)
    return (top, middle, low)


def product_three(exact, values):
    rows = values.shape[0]
    stacked = jnp.concatenate(split_three(values), axis=0)
    found = lax.dot_general(exact, stacked, LAST, preferred_element_type=jnp.float32)
    return found[:, :rows] + found[:, rows : 2 * rows] + found[:, 2 * rows :]


def fused_kernel(
    lens_ref,
    cand_ref,
    text_ref,
    feats_ref,
    states_hbm,
    tproj_hbm,
    query_hbm,
    vproj_hbm,
    sproj_hbm,
    losses_ref,
    grad_ref,
    feats_out_ref,
    states,
    tproj,
    query,
    vproj,
    sproj,
    packs,
    own_rows,
    tokens,
    strong,
    spreads,
    feats_all,
    text_all,
    load_sem,
    send_sem,
    recv_sem,
    spread_send,
    spread_recv,
):
    n_img, n_cap = packs.shape[:2]
    cap_dev, length, width = states.shape
    img_dev, queries = query.shape[:2]
    part_img = img_dev // n_cap
    part_rows = part_img * queries
    itc = tokens.shape[1]
    slots = n_img * n_cap * 8
    text_at, feat_at = (part_rows, part_rows + 32)
    i, j = (lax.axis_index("img"), lax.axis_index("cap"))
    chip, core = (j // 2, j % 2)
    sibling = 2 * chip + (1 - core)
    across = 2 * (1 - chip) + core
    corner = 2 * (1 - chip) + (1 - core)

    loads = []
    for index, (hbm, vmem) in enumerate(
        (
            (query_hbm, query),
            (vproj_hbm, vproj),
            (states_hbm, states),
            (tproj_hbm, tproj),
            (sproj_hbm, sproj),
        )
    ):
        loads.append(pltpu.make_async_copy(hbm, vmem, load_sem.at[index]))
        loads[-1].start()

    barrier = pltpu.get_barrier_semaphore()
    for step in range(1, n_img * n_cap):
        peer = {"img": (i + step // n_cap) % n_img, "cap": (j + step % n_cap) % n_cap}
        pl.semaphore_signal(barrier, inc=1, device_id=peer, device_id_type=MESH)

    def remote(source, target, kind, step, to_img, to_cap):
        return pltpu.make_async_remote_copy(
            src_ref=source,
            dst_ref=target,
            send_sem=send_sem.at[kind, step],
            recv_sem=recv_sem.at[kind, step],
            device_id={"img": to_img, "cap": to_cap},
            device_id_type=MESH,
        )

    mine = packs.at[i, j]
    text = text_ref[...]
    mine[pl.ds(text_at, 16), :] = text[:, :itc]
    mine[pl.ds(text_at + 16, 16), :] = text[:, itc:]
    row = lax.broadcasted_iota(jnp.int32, (n_cap * 8, img_dev), 0)
    column = lax.broadcasted_iota(jnp.int32, (n_cap * 8, img_dev), 1)
    wanted = jnp.where(row % 8 < part_img, (row // 8) * part_img + row % 8, -1)
    chooser = (column == wanted).astype(jnp.bfloat16)
    placed = jnp.dot(chooser, feats_ref[...], preferred_element_type=jnp.float32).astype(
        jnp.bfloat16
    )
    feats_all[pl.ds(pl.multiple_of(i * n_cap * 8, n_cap * 8), n_cap * 8), :] = placed
    for part in range(n_cap):
        begin = itc * min(part, width // itc - 1)

        @pl.when(j == part)
        def _():
            mine[pl.ds(feat_at, 32), :] = placed[:, begin : begin + itc]

    loads[0].wait()
    loads[1].wait()
    own_rows[...] = unit_rows(
        jnp.dot(
            query[...].reshape(img_dev * queries, width),
            vproj[...],
            preferred_element_type=jnp.float32,
        )
    ).astype(jnp.bfloat16)
    mine[pl.ds(0, part_rows), :] = own_rows[
        pl.ds(pl.multiple_of(j * part_rows, part_rows), part_rows), :
    ]
    pl.semaphore_wait(barrier, n_img * n_cap - 1)

    along = {}
    for step in NEAR_FIRST:
        along[step] = remote(mine, mine, 0, step, (i + step) % n_img, j)
        along[step].start()
    texts = {}
    for step, peer in ((1, sibling), (2, across), (3, corner)):
        piece = mine.at[pl.ds(text_at, 32), :]
        texts[step] = remote(piece, piece, 4, step, i, peer)
        texts[step].start()

    loads[2].wait()
    loads[3].wait()
    tokens[...] = unit_rows(
        jnp.dot(
            states[...].reshape(cap_dev * length, width),
            tproj[...],
            preferred_element_type=jnp.float32,
        )
    ).astype(jnp.bfloat16)
    strong[...] = jnp.zeros_like(strong)

    def score(rows, owner, part):
        products = lax.dot_general(rows, tokens[...], LAST, preferred_element_type=jnp.float32)
        strong[owner * n_cap + part, :part_img, :] = jnp.max(
            products.reshape(part_img, queries, cap_dev * length), axis=1
        )

    for part in range(n_cap):
        score(own_rows[pl.ds(part * part_rows, part_rows), :], i, part)

    slot = lax.broadcasted_iota(jnp.int32, (cap_dev, slots), 1)
    image = jnp.where(slot % 8 < part_img, (slot // 8) * part_img + slot % 8, -1)
    counts = jnp.zeros((cap_dev, slots), jnp.float32)
    cand = cand_ref[...]
    for k in range(cand.shape[1]):
        counts += (cand[:, k : k + 1] == image).astype(jnp.float32)
    caption = lax.broadcasted_iota(jnp.int32, (cap_dev, 1), 0)
    lens = jnp.zeros((cap_dev, 1), jnp.int32)
    for c in range(cap_dev):
        lens = jnp.where(caption == c, lens_ref[c], lens)
    place = lax.broadcasted_iota(jnp.int32, (cap_dev, cap_dev * length), 1)
    at = place - caption * length
    mask = ((at >= 0) & (at < lens)).astype(jnp.bfloat16)

    def use_text(owner, part):
        begin = pl.multiple_of((owner * n_cap + part) * 16, 16)
        text_all[pl.ds(begin, 16), :itc] = packs[owner, part, pl.ds(text_at, 16), :]
        text_all[pl.ds(begin, 16), itc:] = packs[owner, part, pl.ds(text_at + 16, 16), :]

    def use(owner, part):
        score(packs[owner, part, pl.ds(0, part_rows), :], owner, part)
        use_text(owner, part)
        rows = pl.ds(pl.multiple_of(owner * n_cap * 8, n_cap * 8), n_cap * 8)
        begin = pl.multiple_of(jnp.minimum(part, width // itc - 1) * itc, itc)
        feats_all[rows, pl.ds(begin, itc)] = packs[owner, part, pl.ds(feat_at, 32), :]

    over, beside, onward = ({}, {}, {})
    for step in NEAR_FIRST:
        owner = (i - step + n_img) % n_img
        along[step].wait_recv()
        block = packs.at[owner, j]
        over[step] = remote(block, block, 1, step, i, across)
        over[step].start()
        beside[step] = remote(block, block, 2, step, i, sibling)
        beside[step].start()
        use(owner, j)
    use_text(i, j)
    for step, peer in ((1, sibling), (2, across), (3, corner)):
        texts[step].wait_recv()
        use_text(i, peer)
    for step in NEAR_FIRST:
        owner = (i - step + n_img) % n_img
        over[step].wait_recv()
        block = packs.at[owner, across]
        onward[step] = remote(block, block, 3, step, i, sibling)
        onward[step].start()
        use(owner, across)
        beside[step].wait_recv()
        use(owner, sibling)
    for step in NEAR_FIRST:
        onward[step].wait_recv()
        use((i - step + n_img) % n_img, corner)

    loads[4].wait()
    embed = jnp.dot(feats_all[...], sproj[...], preferred_element_type=jnp.float32)
    norm = jnp.sqrt(jnp.sum(embed * embed, axis=-1, keepdims=True) + 1e-06)
    unit = embed / norm
    wide = text.astype(jnp.float32)
    text_scale = lax.rsqrt(jnp.sum(wide * wide, axis=-1, keepdims=True) + 1e-06)
    student = LOGIT_SCALE * (product_three(text, unit) * text_scale)
    summed = product_three(mask, strong[...].reshape(slots, cap_dev * length))
    teacher = summed / lens.astype(jnp.float32) / TEACHER_TEMP
    present = counts > 0

    def log_softmax(scores):
        peak = jnp.max(jnp.where(present, scores, -jnp.inf), axis=1, keepdims=True)
        shifted = jnp.where(present, scores - peak, 0.0)
        total = jnp.sum(counts * jnp.exp(shifted), axis=1, keepdims=True)
        return shifted - jnp.log(total)

    teacher_log = log_softmax(teacher)
    student_log = log_softmax(student)
    teacher_prob = jnp.exp(teacher_log)
    spreads[i, j] = (LOGIT_SCALE * text_scale) * (counts * (jnp.exp(student_log) - teacher_prob))
    sent = []
    for step in range(1, n_img * n_cap):
        sent.append(
            pltpu.make_async_remote_copy(
                src_ref=spreads.at[i, j],
                dst_ref=spreads.at[i, j],
                send_sem=spread_send.at[step],
                recv_sem=spread_recv.at[step],
                device_id={
                    "img": (i + step // n_cap) % n_img,
                    "cap": (j + step % n_cap) % n_cap,
                },
                device_id_type=MESH,
            )
        )
        sent[-1].start()
    losses_ref[...] = jnp.sum(
        counts * teacher_prob * (teacher_log - student_log), axis=1, keepdims=True
    )
    turned = feats_all[...].astype(jnp.float32).T.astype(jnp.bfloat16)
    feats_out_ref[:, :slots] = turned
    feats_out_ref[:, slots:] = turned
    for copies in (along, over, beside, onward, texts):
        for step in NEAR_FIRST:
            copies[step].wait_send()
    for copy in sent:
        copy.wait_recv()
    across_captions = spreads[...].reshape(n_img * n_cap * cap_dev, slots).T
    total = jnp.zeros(embed.shape, jnp.float32)
    for piece in split_three(across_captions):
        total += jnp.dot(piece, text_all[...], preferred_element_type=jnp.float32)
    radial = jnp.sum(total * unit, axis=-1, keepdims=True)
    embed_grad = (total - radial * unit) / norm
    top = embed_grad.astype(jnp.bfloat16)
    grad_ref[:slots, :] = top
    grad_ref[slots:, :] = (embed_grad - top.astype(jnp.float32)).astype(jnp.bfloat16)
    for copy in sent:
        copy.wait_send()


def fused(
    text_states,
    text_lens,
    text_proj,
    query_states,
    vision_proj,
    student_text,
    student_feats,
    student_proj,
    candidates,
):
    n_img, n_cap = (lax.axis_size("img"), lax.axis_size("cap"))
    cap_dev, length, width = text_states.shape
    img_dev, queries = query_states.shape[:2]
    itc = text_proj.shape[1]
    embed_width = student_proj.shape[1]
    slots = n_img * n_cap * 8
    part_rows = img_dev * queries // n_cap
    vmem = pl.BlockSpec(memory_space=pltpu.VMEM)
    anywhere = pl.BlockSpec(memory_space=pl.ANY)
    losses, grads, feats = pl.pallas_call(
        fused_kernel,
        out_shape=(
            jax.ShapeDtypeStruct((cap_dev, 1), jnp.float32),
            jax.ShapeDtypeStruct((2 * slots, embed_width), jnp.bfloat16),
            jax.ShapeDtypeStruct((width, 2 * slots), jnp.bfloat16),
        ),
        in_specs=[pl.BlockSpec(memory_space=pltpu.SMEM)] + [vmem] * 3 + [anywhere] * 5,
        out_specs=(vmem, vmem, vmem),
        scratch_shapes=[
            pltpu.VMEM(text_states.shape, jnp.bfloat16),
            pltpu.VMEM(text_proj.shape, jnp.bfloat16),
            pltpu.VMEM(query_states.shape, jnp.bfloat16),
            pltpu.VMEM(vision_proj.shape, jnp.bfloat16),
            pltpu.VMEM(student_proj.shape, jnp.bfloat16),
            pltpu.VMEM((n_img, n_cap, part_rows + 64, itc), jnp.bfloat16),
            pltpu.VMEM((img_dev * queries, itc), jnp.bfloat16),
            pltpu.VMEM((cap_dev * length, itc), jnp.bfloat16),
            pltpu.VMEM((n_img * n_cap, 8, cap_dev * length), jnp.float32),
            pltpu.VMEM((n_img, n_cap, cap_dev, slots), jnp.float32),
            pltpu.VMEM((slots, width), jnp.bfloat16),
            pltpu.VMEM((n_img * n_cap * cap_dev, embed_width), jnp.bfloat16),
            pltpu.SemaphoreType.DMA((5,)),
            pltpu.SemaphoreType.DMA((5, 4)),
            pltpu.SemaphoreType.DMA((5, 4)),
            pltpu.SemaphoreType.DMA((n_img * n_cap,)),
            pltpu.SemaphoreType.DMA((n_img * n_cap,)),
        ],
        compiler_params=pltpu.CompilerParams(
            collective_id=0, has_side_effects=True, vmem_limit_bytes=48 * 1024 * 1024
        ),
    )(
        text_lens,
        candidates,
        student_text,
        student_feats,
        text_states,
        text_proj,
        query_states,
        vision_proj,
        student_proj,
    )
    proj_grad = jnp.dot(feats, grads, preferred_element_type=jnp.float32)
    return (losses.reshape(cap_dev), proj_grad)


def solution(mesh):
    small = mesh.shape["img"] == 4 and mesh.shape["cap"] == 4
    local = fused if small else gathered
    in_specs = (
        P(("groups", "img", "cap"), None, None),
        P(("groups", "img", "cap")),
        P(),
        P(("groups", "img"), None, None),
        P(),
        P(("groups", "img", "cap"), None),
        P(("groups", "img"), None),
        P(),
        P(("groups", "img", "cap"), None),
    )
    out_specs = (P(("groups", "img", "cap")), P("groups", None))
    return jax.shard_map(local, mesh=mesh, in_specs=in_specs, out_specs=out_specs, check_vma=False)
```

```python
import jax
import jax.numpy as jnp
from jax import lax
from jax.experimental import pallas as pl
from jax.experimental.pallas import tpu as pltpu
from jax.sharding import PartitionSpec as P

TEACHER_TEMP = 0.01
LOGIT_SCALE = 100.0
HIGHEST = lax.Precision.HIGHEST


def unit_rows(values):
    return values * lax.rsqrt(jnp.sum(values * values, axis=-1, keepdims=True) + 1e-06)


def gathered(
    text_states,
    text_lens,
    text_proj,
    query_states,
    vision_proj,
    student_text,
    student_feats,
    student_proj,
    candidates,
):
    cap_dev, length, txt_width = text_states.shape
    img_dev = query_states.shape[0]
    query_rows = unit_rows(
        jnp.dot(
            query_states.reshape(-1, txt_width), vision_proj, preferred_element_type=jnp.float32
        )
    ).astype(jnp.bfloat16)
    all_rows = lax.all_gather(query_rows, "img", axis=0, tiled=False)
    all_feats = lax.all_gather(student_feats, "img", axis=0, tiled=True)
    all_text = lax.all_gather(student_text, ("img", "cap"), axis=0, tiled=True)
    token_rows = unit_rows(
        jnp.dot(text_states.reshape(-1, txt_width), text_proj, preferred_element_type=jnp.float32)
    ).astype(jnp.bfloat16)
    img_count = lax.axis_size("img")
    images = img_count * img_dev

    valid_mask = jnp.arange(length)[None, :] < text_lens[:, None]
    pieces = []
    for owner in range(img_count):
        products = jnp.dot(
            token_rows, all_rows[owner].T, preferred_element_type=jnp.float32
        ).reshape(cap_dev, length, img_dev, -1)
        strongest = jnp.max(products, axis=-1)
        pieces.append(jnp.sum(jnp.where(valid_mask[:, :, None], strongest, 0.0), axis=1))
    summed = jnp.concatenate(pieces, axis=1)
    teacher = summed / text_lens[:, None].astype(jnp.float32) / TEACHER_TEMP

    image_embed = jnp.dot(all_feats, student_proj, preferred_element_type=jnp.float32)
    image_norm = jnp.sqrt(jnp.sum(image_embed * image_embed, axis=-1) + 1e-06)
    image_unit = image_embed / image_norm[:, None]
    text_unit = unit_rows(student_text.astype(jnp.float32))
    cosine = jnp.dot(text_unit, image_unit.T, precision=HIGHEST)
    student = LOGIT_SCALE * cosine

    counts = jnp.sum(
        (candidates[:, :, None] == jnp.arange(images)[None, None, :]).astype(jnp.float32), axis=1
    )
    present = counts > 0

    def log_softmax(scores):
        peak = jnp.max(jnp.where(present, scores, -jnp.inf), axis=1, keepdims=True)
        shifted = jnp.where(present, scores - peak, 0.0)
        total = jnp.sum(counts * jnp.exp(shifted), axis=1, keepdims=True)
        return shifted - jnp.log(total)

    teacher_log = log_softmax(teacher)
    student_log = log_softmax(student)
    teacher_prob = jnp.exp(teacher_log)
    losses = jnp.sum(counts * teacher_prob * (teacher_log - student_log), axis=1)
    spread = LOGIT_SCALE * counts * (jnp.exp(student_log) - teacher_prob)
    radial = jnp.sum(spread * cosine, axis=0, keepdims=True)
    all_spread = lax.all_gather(
        jnp.concatenate([spread, radial], axis=0), ("img", "cap"), axis=0, tiled=False
    )
    radial = jnp.sum(all_spread[:, cap_dev], axis=0)
    all_spread = all_spread[:, :cap_dev].reshape(-1, images)
    all_unit = unit_rows(all_text.astype(jnp.float32))
    embed_grad = (
        jnp.einsum("ci,cd->id", all_spread, all_unit, precision=HIGHEST)
        - radial[:, None] * image_unit
    ) / image_norm[:, None]
    top = lax.optimization_barrier(embed_grad.astype(jnp.bfloat16))
    rest = (embed_grad - top.astype(jnp.float32)).astype(jnp.bfloat16)
    proj_grad = jnp.einsum(
        "is,id->sd",
        jnp.concatenate([all_feats, all_feats], axis=0),
        jnp.concatenate([top, rest], axis=0),
        preferred_element_type=jnp.float32,
    )
    return (losses, proj_grad)


MESH = pl.DeviceIdType.MESH
LAST = (((1,), (1,)), ((), ()))
STEPS = (1, 2, 3)


def split_three(values):
    top = values.astype(jnp.bfloat16)
    rest = values - top.astype(jnp.float32)
    middle = rest.astype(jnp.bfloat16)
    low = (rest - middle.astype(jnp.float32)).astype(jnp.bfloat16)
    return (top, middle, low)


def product_three(exact, values):
    rows = values.shape[0]
    stacked = jnp.concatenate(split_three(values), axis=0)
    found = lax.dot_general(exact, stacked, LAST, preferred_element_type=jnp.float32)
    return found[:, :rows] + found[:, rows : 2 * rows] + found[:, 2 * rows :]


def fused_kernel(
    states_hbm,
    lens_hbm,
    tproj_hbm,
    query_hbm,
    vproj_hbm,
    text_hbm,
    feats_hbm,
    sproj_hbm,
    cand_hbm,
    losses_ref,
    grad_ref,
    feats_out_ref,
    states,
    lens_ref,
    tproj,
    query,
    vproj,
    text_ref,
    feats_ref,
    sproj,
    cand_ref,
    quarter,
    packs,
    sides,
    own_rows,
    tokens,
    strong,
    spreads,
    feats_all,
    text_all,
    load_sem,
    send_sem,
    recv_sem,
    spread_send,
    spread_recv,
):
    n_img, n_cap = packs.shape[:2]
    cap_dev, length, width = states.shape
    img_dev, queries = query.shape[:2]
    part_img = img_dev // n_cap
    part_rows = part_img * queries
    itc = tokens.shape[1]
    slots = n_img * n_cap * 8
    i, j = (lax.axis_index("img"), lax.axis_index("cap"))
    chip, core = (j // 2, j % 2)
    sibling = 2 * chip + (1 - core)
    across = 2 * (1 - chip) + core
    corner = 2 * (1 - chip) + (1 - core)
    mates = ((1, sibling), (2, across), (3, corner))
    level = {1: i + 1 - 2 * (i % 2), 2: (i + 2) % n_img, 3: n_img - 1 - i}

    barrier = pltpu.get_barrier_semaphore()
    for step in range(1, n_img * n_cap):
        peer = {"img": (i + step // n_cap) % n_img, "cap": (j + step % n_cap) % n_cap}
        pl.semaphore_signal(barrier, inc=1, device_id=peer, device_id_type=MESH)

    loads = {}
    for index, (name, hbm, vmem) in enumerate(
        (
            ("text", text_hbm, text_ref),
            ("feats", feats_hbm, feats_ref),
            ("quarter", query_hbm.at[pl.ds(j * part_img, part_img)], quarter),
            ("vproj", vproj_hbm, vproj),
            ("tproj", tproj_hbm, tproj),
            ("states", states_hbm, states),
            ("query", query_hbm, query),
            ("cand", cand_hbm, cand_ref),
            ("lens", lens_hbm, lens_ref),
            ("sproj", sproj_hbm, sproj),
        )
    ):
        loads[name] = pltpu.make_async_copy(hbm, vmem, load_sem.at[index])
        loads[name].start()

    def remote(block, kind, step, to_img, to_cap):
        copy = pltpu.make_async_remote_copy(
            src_ref=block,
            dst_ref=block,
            send_sem=send_sem.at[kind, step],
            recv_sem=recv_sem.at[kind, step],
            device_id={"img": to_img, "cap": to_cap},
            device_id_type=MESH,
        )
        copy.start()
        return copy

    mine, side = (packs.at[i, j], sides.at[i, j])
    loads["text"].wait()
    loads["feats"].wait()
    text = text_ref[...]
    side[pl.ds(0, 16), :] = text[:, :itc]
    side[pl.ds(16, 16), :] = text[:, itc:]
    row = lax.broadcasted_iota(jnp.int32, (n_cap * 8, img_dev), 0)
    column = lax.broadcasted_iota(jnp.int32, (n_cap * 8, img_dev), 1)
    wanted = jnp.where(row % 8 < part_img, (row // 8) * part_img + row % 8, -1)
    chooser = (column == wanted).astype(jnp.bfloat16)
    placed = jnp.dot(chooser, feats_ref[...], preferred_element_type=jnp.float32).astype(
        jnp.bfloat16
    )
    feats_all[pl.ds(pl.multiple_of(i * n_cap * 8, n_cap * 8), n_cap * 8), :] = placed
    for part in range(n_cap):
        begin = itc * min(part, width // itc - 1)

        @pl.when(j == part)
        def _():
            side[pl.ds(32, 32), :] = placed[:, begin : begin + itc]

    pl.semaphore_wait(barrier, n_img * n_cap - 1)
    side_along = {step: remote(side, 0, step, level[step], j) for step in STEPS}
    texts = {
        step: remote(side.at[pl.ds(0, 32), :], 1, step, i, peer) for step, peer in mates
    }

    def rows_of(values):
        return unit_rows(
            jnp.dot(
                values.reshape(-1, width), vproj[...], preferred_element_type=jnp.float32
            )
        ).astype(jnp.bfloat16)

    loads["quarter"].wait()
    loads["vproj"].wait()
    mine[...] = rows_of(quarter[...])
    along = {step: remote(mine, 2, step, level[step], j) for step in STEPS}

    loads["states"].wait()
    loads["tproj"].wait()
    tokens[...] = unit_rows(
        jnp.dot(
            states[...].reshape(cap_dev * length, width),
            tproj[...],
            preferred_element_type=jnp.float32,
        )
    ).astype(jnp.bfloat16)
    strong[...] = jnp.zeros_like(strong)

    side_over, side_beside, side_onward = ({}, {}, {})
    for step in STEPS:
        side_along[step].wait_recv()
        block = sides.at[level[step], j]
        side_over[step] = remote(block, 3, step, i, across)
        side_beside[step] = remote(block, 4, step, i, sibling)

    def score(rows, owner, part):
        products = lax.dot_general(rows, tokens[...], LAST, preferred_element_type=jnp.float32)
        strong[owner * n_cap + part, :part_img, :] = jnp.max(
            products.reshape(part_img, queries, cap_dev * length), axis=1
        )

    loads["query"].wait()
    own_rows[...] = rows_of(query[...])
    for part in range(n_cap):
        score(own_rows[pl.ds(part * part_rows, part_rows), :], i, part)

    def use(owner, part):
        score(packs[owner, part], owner, part)

    over, beside, onward = ({}, {}, {})

    def pass_on(step):
        along[step].wait_recv()
        block = packs.at[level[step], j]
        over[step] = remote(block, 6, step, i, across)
        beside[step] = remote(block, 7, step, i, sibling)
        use(level[step], j)

    pass_on(1)
    for step in STEPS:
        side_over[step].wait_recv()
        side_onward[step] = remote(sides.at[level[step], across], 5, step, i, sibling)

    loads["cand"].wait()
    slot = lax.broadcasted_iota(jnp.int32, (cap_dev, slots), 1)
    image = jnp.where(slot % 8 < part_img, (slot // 8) * part_img + slot % 8, -1)
    counts = jnp.zeros((cap_dev, slots), jnp.float32)
    cand = cand_ref[...]
    for k in range(cand.shape[1]):
        counts += (cand[:, k : k + 1] == image).astype(jnp.float32)
    present = counts > 0
    loads["lens"].wait()
    caption = lax.broadcasted_iota(jnp.int32, (cap_dev, 1), 0)
    lens = jnp.zeros((cap_dev, 1), jnp.int32)
    for c in range(cap_dev):
        lens = jnp.where(caption == c, lens_ref[c], lens)
    place = lax.broadcasted_iota(jnp.int32, (cap_dev, cap_dev * length), 1)
    at = place - caption * length
    mask = ((at >= 0) & (at < lens)).astype(jnp.bfloat16)

    pass_on(2)

    def use_text(owner, part):
        begin = pl.multiple_of((owner * n_cap + part) * 16, 16)
        text_all[pl.ds(begin, 16), :itc] = sides[owner, part, pl.ds(0, 16), :]
        text_all[pl.ds(begin, 16), itc:] = sides[owner, part, pl.ds(16, 16), :]

    def use_side(owner, part):
        use_text(owner, part)
        rows = pl.ds(pl.multiple_of(owner * n_cap * 8, n_cap * 8), n_cap * 8)
        begin = pl.multiple_of(jnp.minimum(part, width // itc - 1) * itc, itc)
        feats_all[rows, pl.ds(begin, itc)] = sides[owner, part, pl.ds(32, 32), :]

    use_text(i, j)
    for step, peer in mates:
        texts[step].wait_recv()
        use_text(i, peer)
    for step in STEPS:
        use_side(level[step], j)
        use_side(level[step], across)
        side_beside[step].wait_recv()
        use_side(level[step], sibling)
        side_onward[step].wait_recv()
        use_side(level[step], corner)

    def log_softmax(scores):
        peak = jnp.max(jnp.where(present, scores, -jnp.inf), axis=1, keepdims=True)
        shifted = jnp.where(present, scores - peak, 0.0)
        total = jnp.sum(counts * jnp.exp(shifted), axis=1, keepdims=True)
        return shifted - jnp.log(total)

    loads["sproj"].wait()
    embed = jnp.dot(feats_all[...], sproj[...], preferred_element_type=jnp.float32)
    norm = jnp.sqrt(jnp.sum(embed * embed, axis=-1, keepdims=True) + 1e-06)
    unit = embed / norm
    wide = text.astype(jnp.float32)
    text_scale = lax.rsqrt(jnp.sum(wide * wide, axis=-1, keepdims=True) + 1e-06)
    student_log = log_softmax(LOGIT_SCALE * (product_three(text, unit) * text_scale))
    student_prob = jnp.exp(student_log)
    turned = feats_all[...].astype(jnp.float32).T.astype(jnp.bfloat16)
    feats_out_ref[:, :slots] = turned
    feats_out_ref[:, slots:] = turned

    pass_on(3)
    for step in STEPS:
        over[step].wait_recv()
        onward[step] = remote(packs.at[level[step], across], 8, step, i, sibling)
        beside[step].wait_recv()
        use(level[step], sibling)
        use(level[step], across)
    for step in STEPS:
        onward[step].wait_recv()
        use(level[step], corner)

    summed = product_three(mask, strong[...].reshape(slots, cap_dev * length))
    teacher_log = log_softmax(summed / lens.astype(jnp.float32) / TEACHER_TEMP)
    teacher_prob = jnp.exp(teacher_log)
    spreads[i, j] = (LOGIT_SCALE * text_scale) * (counts * (student_prob - teacher_prob))
    sent = []
    for step in range(1, n_img * n_cap):
        sent.append(
            pltpu.make_async_remote_copy(
                src_ref=spreads.at[i, j],
                dst_ref=spreads.at[i, j],
                send_sem=spread_send.at[step],
                recv_sem=spread_recv.at[step],
                device_id={
                    "img": (i + step // n_cap) % n_img,
                    "cap": (j + step % n_cap) % n_cap,
                },
                device_id_type=MESH,
            )
        )
        sent[-1].start()
    terms = counts * teacher_prob * (teacher_log - student_log)
    losses_ref[...] = jnp.sum(terms.T, axis=0, keepdims=True)
    for copies in (
        side_along, side_over, side_beside, side_onward, along, over, beside, onward, texts
    ):
        for step in STEPS:
            copies[step].wait_send()
    for copy in sent:
        copy.wait_recv()
    across_captions = spreads[...].reshape(n_img * n_cap * cap_dev, slots).T
    total = jnp.zeros(embed.shape, jnp.float32)
    for piece in split_three(across_captions):
        total += jnp.dot(piece, text_all[...], preferred_element_type=jnp.float32)
    radial = jnp.sum(total * unit, axis=-1, keepdims=True)
    embed_grad = (total - radial * unit) / norm
    top = embed_grad.astype(jnp.bfloat16)
    grad_ref[:slots, :] = top
    grad_ref[slots:, :] = (embed_grad - top.astype(jnp.float32)).astype(jnp.bfloat16)
    for copy in sent:
        copy.wait_send()


def fused(
    text_states,
    text_lens,
    text_proj,
    query_states,
    vision_proj,
    student_text,
    student_feats,
    student_proj,
    candidates,
):
    n_img, n_cap = (lax.axis_size("img"), lax.axis_size("cap"))
    cap_dev, length, width = text_states.shape
    img_dev, queries = query_states.shape[:2]
    itc = text_proj.shape[1]
    embed_width = student_proj.shape[1]
    slots = n_img * n_cap * 8
    part_img = img_dev // n_cap
    vmem = pl.BlockSpec(memory_space=pltpu.VMEM)
    args = (
        text_states,
        text_lens,
        text_proj,
        query_states,
        vision_proj,
        student_text,
        student_feats,
        student_proj,
        candidates,
    )
    held = [pltpu.VMEM(arg.shape, arg.dtype) for arg in args]
    held[1] = pltpu.SMEM(text_lens.shape, text_lens.dtype)
    losses, grads, feats = pl.pallas_call(
        fused_kernel,
        out_shape=(
            jax.ShapeDtypeStruct((1, cap_dev), jnp.float32),
            jax.ShapeDtypeStruct((2 * slots, embed_width), jnp.bfloat16),
            jax.ShapeDtypeStruct((width, 2 * slots), jnp.bfloat16),
        ),
        in_specs=[pl.BlockSpec(memory_space=pltpu.HBM)] * len(args),
        out_specs=(vmem, vmem, vmem),
        scratch_shapes=held
        + [
            pltpu.VMEM((part_img, queries, width), jnp.bfloat16),
            pltpu.VMEM((n_img, n_cap, part_img * queries, itc), jnp.bfloat16),
            pltpu.VMEM((n_img, n_cap, 64, itc), jnp.bfloat16),
            pltpu.VMEM((img_dev * queries, itc), jnp.bfloat16),
            pltpu.VMEM((cap_dev * length, itc), jnp.bfloat16),
            pltpu.VMEM((n_img * n_cap, 8, cap_dev * length), jnp.float32),
            pltpu.VMEM((n_img, n_cap, cap_dev, slots), jnp.float32),
            pltpu.VMEM((slots, width), jnp.bfloat16),
            pltpu.VMEM((n_img * n_cap * cap_dev, embed_width), jnp.bfloat16),
            pltpu.SemaphoreType.DMA((10,)),
            pltpu.SemaphoreType.DMA((9, 4)),
            pltpu.SemaphoreType.DMA((9, 4)),
            pltpu.SemaphoreType.DMA((n_img * n_cap,)),
            pltpu.SemaphoreType.DMA((n_img * n_cap,)),
        ],
        compiler_params=pltpu.CompilerParams(
            collective_id=0, has_side_effects=True, vmem_limit_bytes=60 * 1024 * 1024
        ),
    )(*args)
    proj_grad = jnp.dot(feats, grads, preferred_element_type=jnp.float32)
    return (losses.reshape(cap_dev), proj_grad)


def solution(mesh):
    small = mesh.shape["img"] == 4 and mesh.shape["cap"] == 4
    local = fused if small else gathered
    in_specs = (
        P(("groups", "img", "cap"), None, None),
        P(("groups", "img", "cap")),
        P(),
        P(("groups", "img"), None, None),
        P(),
        P(("groups", "img", "cap"), None),
        P(("groups", "img"), None),
        P(),
        P(("groups", "img", "cap"), None),
    )
    out_specs = (P(("groups", "img", "cap")), P("groups", None))
    return jax.shard_map(local, mesh=mesh, in_specs=in_specs, out_specs=out_specs, check_vma=False)
```

```python
import jax
import jax.numpy as jnp
from jax import lax
from jax.experimental import pallas as pl
from jax.experimental.pallas import tpu as pltpu
from jax.sharding import PartitionSpec as P

TEACHER_TEMP = 0.01
LOGIT_SCALE = 100.0
HIGHEST = lax.Precision.HIGHEST


def unit_rows(values):
    return values * lax.rsqrt(jnp.sum(values * values, axis=-1, keepdims=True) + 1e-06)


def gathered(
    text_states,
    text_lens,
    text_proj,
    query_states,
    vision_proj,
    student_text,
    student_feats,
    student_proj,
    candidates,
):
    cap_dev, length, txt_width = text_states.shape
    img_dev = query_states.shape[0]
    query_rows = unit_rows(
        jnp.dot(
            query_states.reshape(-1, txt_width), vision_proj, preferred_element_type=jnp.float32
        )
    ).astype(jnp.bfloat16)
    all_rows = lax.all_gather(query_rows, "img", axis=0, tiled=False)
    all_feats = lax.all_gather(student_feats, "img", axis=0, tiled=True)
    all_text = lax.all_gather(student_text, ("img", "cap"), axis=0, tiled=True)
    token_rows = unit_rows(
        jnp.dot(text_states.reshape(-1, txt_width), text_proj, preferred_element_type=jnp.float32)
    ).astype(jnp.bfloat16)
    img_count = lax.axis_size("img")
    images = img_count * img_dev

    valid_mask = jnp.arange(length)[None, :] < text_lens[:, None]
    pieces = []
    for owner in range(img_count):
        products = jnp.dot(
            token_rows, all_rows[owner].T, preferred_element_type=jnp.float32
        ).reshape(cap_dev, length, img_dev, -1)
        strongest = jnp.max(products, axis=-1)
        pieces.append(jnp.sum(jnp.where(valid_mask[:, :, None], strongest, 0.0), axis=1))
    summed = jnp.concatenate(pieces, axis=1)
    teacher = summed / text_lens[:, None].astype(jnp.float32) / TEACHER_TEMP

    image_embed = jnp.dot(all_feats, student_proj, preferred_element_type=jnp.float32)
    image_norm = jnp.sqrt(jnp.sum(image_embed * image_embed, axis=-1) + 1e-06)
    image_unit = image_embed / image_norm[:, None]
    text_unit = unit_rows(student_text.astype(jnp.float32))
    cosine = jnp.dot(text_unit, image_unit.T, precision=HIGHEST)
    student = LOGIT_SCALE * cosine

    counts = jnp.sum(
        (candidates[:, :, None] == jnp.arange(images)[None, None, :]).astype(jnp.float32), axis=1
    )
    present = counts > 0

    def log_softmax(scores):
        peak = jnp.max(jnp.where(present, scores, -jnp.inf), axis=1, keepdims=True)
        shifted = jnp.where(present, scores - peak, 0.0)
        total = jnp.sum(counts * jnp.exp(shifted), axis=1, keepdims=True)
        return shifted - jnp.log(total)

    teacher_log = log_softmax(teacher)
    student_log = log_softmax(student)
    teacher_prob = jnp.exp(teacher_log)
    losses = jnp.sum(counts * teacher_prob * (teacher_log - student_log), axis=1)
    spread = LOGIT_SCALE * counts * (jnp.exp(student_log) - teacher_prob)
    radial = jnp.sum(spread * cosine, axis=0, keepdims=True)
    all_spread = lax.all_gather(
        jnp.concatenate([spread, radial], axis=0), ("img", "cap"), axis=0, tiled=False
    )
    radial = jnp.sum(all_spread[:, cap_dev], axis=0)
    all_spread = all_spread[:, :cap_dev].reshape(-1, images)
    all_unit = unit_rows(all_text.astype(jnp.float32))
    embed_grad = (
        jnp.einsum("ci,cd->id", all_spread, all_unit, precision=HIGHEST)
        - radial[:, None] * image_unit
    ) / image_norm[:, None]
    top = lax.optimization_barrier(embed_grad.astype(jnp.bfloat16))
    rest = (embed_grad - top.astype(jnp.float32)).astype(jnp.bfloat16)
    proj_grad = jnp.einsum(
        "is,id->sd",
        jnp.concatenate([all_feats, all_feats], axis=0),
        jnp.concatenate([top, rest], axis=0),
        preferred_element_type=jnp.float32,
    )
    return (losses, proj_grad)


MESH = pl.DeviceIdType.MESH
LAST = (((1,), (1,)), ((), ()))
STEPS = (1, 2, 3)
CHUNKS = 1


def split_three(values):
    top = values.astype(jnp.bfloat16)
    rest = values - top.astype(jnp.float32)
    middle = rest.astype(jnp.bfloat16)
    low = (rest - middle.astype(jnp.float32)).astype(jnp.bfloat16)
    return (top, middle, low)


def product_three(exact, values):
    rows = values.shape[0]
    stacked = jnp.concatenate(split_three(values), axis=0)
    found = lax.dot_general(exact, stacked, LAST, preferred_element_type=jnp.float32)
    return found[:, :rows] + found[:, rows : 2 * rows] + found[:, 2 * rows :]


def fused_kernel(
    states_hbm,
    lens_hbm,
    tproj_hbm,
    query_hbm,
    vproj_hbm,
    text_hbm,
    feats_hbm,
    sproj_hbm,
    cand_hbm,
    losses_ref,
    grad_ref,
    feats_out_ref,
    states,
    lens_ref,
    tproj,
    query,
    vproj,
    text_ref,
    feats_ref,
    sproj,
    cand_ref,
    quarter,
    packs,
    side_parts,
    own_rows,
    tokens,
    strong,
    spreads,
    feats_all,
    text_all,
    load_sem,
    send_sem,
    recv_sem,
    spread_send,
    spread_recv,
):
    n_img, n_cap = packs.shape[:2]
    cap_dev, length, width = states.shape
    img_dev, queries = query.shape[:2]
    part_img = img_dev // n_cap
    part_rows = part_img * queries
    itc = tokens.shape[1]
    slots = n_img * n_cap * 8
    i, j = (lax.axis_index("img"), lax.axis_index("cap"))
    chip, core = (j // 2, j % 2)
    sibling = 2 * chip + (1 - core)
    across = 2 * (1 - chip) + core
    corner = 2 * (1 - chip) + (1 - core)
    mates = ((1, sibling), (2, across))
    level = {0: i, 1: i + 1 - 2 * (i % 2), 2: (i + 2) % n_img, 3: n_img - 1 - i}

    barrier = pltpu.get_barrier_semaphore()
    for to_img, to_cap in ((level[1], j), (level[2], j), (i, sibling), (i, across)):
        pl.semaphore_signal(
            barrier, inc=1, device_id={"img": to_img, "cap": to_cap}, device_id_type=MESH
        )

    loads = {}
    for index, (name, hbm, vmem) in enumerate(
        (
            ("text", text_hbm, text_ref),
            ("feats", feats_hbm, feats_ref),
            ("quarter", query_hbm.at[pl.ds(j * part_img, part_img)], quarter),
            ("vproj", vproj_hbm, vproj),
            ("tproj", tproj_hbm, tproj),
            ("states", states_hbm, states),
            ("query", query_hbm, query),
            ("cand", cand_hbm, cand_ref),
            ("lens", lens_hbm, lens_ref),
            ("sproj", sproj_hbm, sproj),
        )
    ):
        loads[name] = pltpu.make_async_copy(hbm, vmem, load_sem.at[index])
        loads[name].start()

    def remote(block, stream, kind, step, to_img, to_cap):
        copy = pltpu.make_async_remote_copy(
            src_ref=block,
            dst_ref=block,
            send_sem=send_sem.at[stream, kind, step],
            recv_sem=recv_sem.at[stream, kind, step],
            device_id={"img": to_img, "cap": to_cap},
            device_id_type=MESH,
        )
        copy.start()
        return copy

    class Stream:
        def __init__(self, index, block):
            self.index, self.block = (index, block)
            self.along, self.over, self.beside, self.onward = ({}, {}, {}, {})

        def start(self):
            for step in (2, 1):
                self.along[step] = remote(self.block(i, j), self.index, 0, step, level[step], j)

        def pass_on(self, step):
            self.along[step].wait_recv()
            block = self.block(level[step], j)
            if step == 2:
                self.along[3] = remote(block, self.index, 0, 3, level[1], j)
            self.over[step] = remote(block, self.index, 1, step, i, across)
            self.beside[step] = remote(block, self.index, 2, step, i, sibling)

        def turn(self, step):
            self.over[step].wait_recv()
            self.onward[step] = remote(
                self.block(level[step], across), self.index, 3, step, i, sibling
            )

        def sent(self):
            for copies in (self.along, self.over, self.beside, self.onward):
                for step in STEPS:
                    copies[step].wait_send()

    chunk_img = part_img // CHUNKS
    chunk_rows = chunk_img * queries
    side_stream = Stream(0, lambda owner, part: side_parts.at[owner, part])

    def chunk_of(chunk):
        return lambda owner, part: packs.at[
            owner, part, pl.ds(chunk * chunk_rows, chunk_rows), :
        ]

    row_streams = [Stream(1 + chunk, chunk_of(chunk)) for chunk in range(CHUNKS)]

    loads["text"].wait()
    loads["feats"].wait()
    text = text_ref[...]
    side_parts[i, j, 32:48, :] = text[:, :itc]
    side_parts[i, j, 48:, :] = text[:, itc:]
    row = lax.broadcasted_iota(jnp.int32, (n_cap * 8, img_dev), 0)
    column = lax.broadcasted_iota(jnp.int32, (n_cap * 8, img_dev), 1)
    wanted = jnp.where(row % 8 < part_img, (row // 8) * part_img + row % 8, -1)
    chooser = (column == wanted).astype(jnp.bfloat16)
    placed = jnp.dot(chooser, feats_ref[...], preferred_element_type=jnp.float32).astype(
        jnp.bfloat16
    )
    feats_all[pl.ds(pl.multiple_of(i * n_cap * 8, n_cap * 8), n_cap * 8), :] = placed
    for part in range(n_cap):
        begin = itc * min(part, width // itc - 1)

        @pl.when(j == part)
        def _():
            side_parts[i, j, :32, :] = placed[:, begin : begin + itc]

    pl.semaphore_wait(barrier, 4)
    side_stream.start()

    def own_text(part, step, to_cap):
        block = side_parts.at[i, part, pl.ds(32, 32), :]
        return remote(block, 1 + CHUNKS, 0, step, i, to_cap)

    texts = {step: own_text(j, step, peer) for step, peer in mates}

    def rows_of(values):
        return unit_rows(
            jnp.dot(
                values.reshape(-1, width), vproj[...], preferred_element_type=jnp.float32
            )
        ).astype(jnp.bfloat16)

    loads["quarter"].wait()
    loads["vproj"].wait()
    for chunk in range(CHUNKS):
        packs[i, j, pl.ds(chunk * chunk_rows, chunk_rows), :] = rows_of(
            quarter[pl.ds(chunk * chunk_img, chunk_img)]
        )
        row_streams[chunk].start()
    loads["states"].wait()
    loads["tproj"].wait()
    tokens[...] = unit_rows(
        jnp.dot(
            states[...].reshape(cap_dev * length, width),
            tproj[...],
            preferred_element_type=jnp.float32,
        )
    ).astype(jnp.bfloat16)
    strong[...] = jnp.zeros_like(strong)

    def score(rows, owner, part, at, count):
        products = lax.dot_general(rows, tokens[...], LAST, preferred_element_type=jnp.float32)
        strong[owner * n_cap + part, at : at + count, :] = jnp.max(
            products.reshape(count, queries, cap_dev * length), axis=1
        )

    def use(owner, part, chunk):
        score(chunk_of(chunk)(owner, part)[...], owner, part, chunk * chunk_img, chunk_img)

    def use_text(owner, part):
        begin = pl.multiple_of((owner * n_cap + part) * 16, 16)
        text_all[pl.ds(begin, 16), :itc] = side_parts[owner, part, 32:48, :]
        text_all[pl.ds(begin, 16), itc:] = side_parts[owner, part, 48:, :]

    def use_feats(owner, part):
        rows = pl.ds(pl.multiple_of(owner * n_cap * 8, n_cap * 8), n_cap * 8)
        begin = pl.multiple_of(jnp.minimum(part, width // itc - 1) * itc, itc)
        feats_all[rows, pl.ds(begin, itc)] = side_parts[owner, part, :32, :]

    def log_softmax(scores):
        peak = jnp.max(jnp.where(present, scores, -jnp.inf), axis=1, keepdims=True)
        shifted = jnp.where(present, scores - peak, 0.0)
        total = jnp.sum(counts * jnp.exp(shifted), axis=1, keepdims=True)
        return shifted - jnp.log(total)

    def forward(step):
        for chunk in range(CHUNKS):
            row_streams[chunk].pass_on(step)

    def score_block(owner, part):
        for chunk in range(CHUNKS):
            use(owner, part, chunk)

    side_stream.pass_on(1)
    side_stream.pass_on(2)
    forward(1)
    forward(2)
    loads["query"].wait()
    own_rows[...] = rows_of(query[...])
    for part in range(n_cap):
        score(own_rows[pl.ds(part * part_rows, part_rows), :], i, part, 0, part_img)
    score_block(level[1], j)
    side_stream.pass_on(3)
    forward(3)
    score_block(level[2], j)
    score_block(level[3], j)
    loads["cand"].wait()
    slot = lax.broadcasted_iota(jnp.int32, (cap_dev, slots), 1)
    image = jnp.where(slot % 8 < part_img, (slot // 8) * part_img + slot % 8, -1)
    counts = jnp.zeros((cap_dev, slots), jnp.float32)
    cand = cand_ref[...]
    for k in range(cand.shape[1]):
        counts += (cand[:, k : k + 1] == image).astype(jnp.float32)
    present = counts > 0
    loads["lens"].wait()
    caption = lax.broadcasted_iota(jnp.int32, (cap_dev, 1), 0)
    lens = jnp.zeros((cap_dev, 1), jnp.int32)
    for c in range(cap_dev):
        lens = jnp.where(caption == c, lens_ref[c], lens)
    place = lax.broadcasted_iota(jnp.int32, (cap_dev, cap_dev * length), 1)
    at = place - caption * length
    mask = ((at >= 0) & (at < lens)).astype(jnp.bfloat16)
    for step in STEPS:
        for chunk in range(CHUNKS):
            row_streams[chunk].turn(step)
        side_stream.turn(step)
        if step == 1:
            texts[2].wait_recv()
            texts[3] = own_text(across, 3, sibling)
        if step < 3:
            for chunk in range(CHUNKS):
                row_streams[chunk].beside[step].wait_recv()
                use(level[step], sibling, chunk)
                use(level[step], across, chunk)
    score_block(level[3], across)
    for chunk in range(CHUNKS):
        row_streams[chunk].beside[3].wait_recv()
        use(level[3], sibling, chunk)
    for step in STEPS:
        use_feats(level[step], j)
        use_feats(level[step], across)
        side_stream.beside[step].wait_recv()
        use_feats(level[step], sibling)
        side_stream.onward[step].wait_recv()
        use_feats(level[step], corner)
    loads["sproj"].wait()
    embed = jnp.dot(feats_all[...], sproj[...], preferred_element_type=jnp.float32)
    norm = jnp.sqrt(jnp.sum(embed * embed, axis=-1, keepdims=True) + 1e-06)
    unit = embed / norm
    wide = text.astype(jnp.float32)
    text_scale = lax.rsqrt(jnp.sum(wide * wide, axis=-1, keepdims=True) + 1e-06)
    student_log = log_softmax(LOGIT_SCALE * (product_three(text, unit) * text_scale))
    student_prob = jnp.exp(student_log)
    turned = feats_all[...].astype(jnp.float32).T.astype(jnp.bfloat16)
    feats_out_ref[:, :slots] = turned
    feats_out_ref[:, slots:] = turned
    for step in STEPS:
        for chunk in range(CHUNKS):
            row_streams[chunk].onward[step].wait_recv()
            use(level[step], corner, chunk)

    summed = product_three(mask, strong[...].reshape(slots, cap_dev * length))
    teacher_log = log_softmax(summed / lens.astype(jnp.float32) / TEACHER_TEMP)
    teacher_prob = jnp.exp(teacher_log)
    spreads[i, j] = (LOGIT_SCALE * text_scale) * (counts * (student_prob - teacher_prob))
    def spread_copy(block, index, to_img, to_cap):
        copy = pltpu.make_async_remote_copy(
            src_ref=block,
            dst_ref=block,
            send_sem=spread_send.at[index],
            recv_sem=spread_recv.at[index],
            device_id={"img": to_img, "cap": to_cap},
            device_id_type=MESH,
        )
        copy.start()
        return copy

    direct = {
        2 * step + side: spread_copy(
            spreads.at[i, j], 2 * step + side, level[step], across if side else j
        )
        for step, side in ((3, 1), (3, 0), (2, 1), (2, 0), (1, 1), (1, 0), (0, 1))
    }
    relayed = [spread_copy(spreads.at[i, j], 8, i, sibling)]
    terms = counts * teacher_prob * (teacher_log - student_log)
    losses_ref[...] = jnp.sum(terms.T, axis=0, keepdims=True)
    use_text(i, j)
    use_text(i, across)
    texts[1].wait_recv()
    use_text(i, sibling)
    texts[3].wait_recv()
    use_text(i, corner)
    for step in STEPS:
        use_text(level[step], j)
        use_text(level[step], across)
        use_text(level[step], sibling)
        use_text(level[step], corner)
    for step, side in ((0, 1), (1, 0), (1, 1), (2, 0), (2, 1), (3, 0), (3, 1)):
        direct[2 * step + side].wait_recv()
        relayed.append(
            spread_copy(
                spreads.at[level[step], across if side else j],
                8 + 2 * step + side,
                i,
                sibling,
            )
        )
    for stream in [side_stream] + row_streams:
        stream.sent()
    for step in STEPS:
        texts[step].wait_send()
    for copy in relayed:
        copy.wait_recv()
    across_captions = spreads[...].reshape(n_img * n_cap * cap_dev, slots).T
    total = jnp.zeros(embed.shape, jnp.float32)
    for piece in split_three(across_captions):
        total += jnp.dot(piece, text_all[...], preferred_element_type=jnp.float32)
    radial = jnp.sum(total * unit, axis=-1, keepdims=True)
    embed_grad = (total - radial * unit) / norm
    top = embed_grad.astype(jnp.bfloat16)
    grad_ref[:slots, :] = top
    grad_ref[slots:, :] = (embed_grad - top.astype(jnp.float32)).astype(jnp.bfloat16)
    for copy in list(direct.values()) + relayed:
        copy.wait_send()


def fused(
    text_states,
    text_lens,
    text_proj,
    query_states,
    vision_proj,
    student_text,
    student_feats,
    student_proj,
    candidates,
):
    n_img, n_cap = (lax.axis_size("img"), lax.axis_size("cap"))
    cap_dev, length, width = text_states.shape
    img_dev, queries = query_states.shape[:2]
    itc = text_proj.shape[1]
    embed_width = student_proj.shape[1]
    slots = n_img * n_cap * 8
    part_img = img_dev // n_cap
    vmem = pl.BlockSpec(memory_space=pltpu.VMEM)
    args = (
        text_states,
        text_lens,
        text_proj,
        query_states,
        vision_proj,
        student_text,
        student_feats,
        student_proj,
        candidates,
    )
    held = [pltpu.VMEM(arg.shape, arg.dtype) for arg in args]
    held[1] = pltpu.SMEM(text_lens.shape, text_lens.dtype)
    losses, grads, feats = pl.pallas_call(
        fused_kernel,
        out_shape=(
            jax.ShapeDtypeStruct((1, cap_dev), jnp.float32),
            jax.ShapeDtypeStruct((2 * slots, embed_width), jnp.bfloat16),
            jax.ShapeDtypeStruct((width, 2 * slots), jnp.bfloat16),
        ),
        in_specs=[pl.BlockSpec(memory_space=pltpu.HBM)] * len(args),
        out_specs=(vmem, vmem, vmem),
        scratch_shapes=held
        + [
            pltpu.VMEM((part_img, queries, width), jnp.bfloat16),
            pltpu.VMEM((n_img, n_cap, part_img * queries, itc), jnp.bfloat16),
            pltpu.VMEM((n_img, n_cap, 64, itc), jnp.bfloat16),
            pltpu.VMEM((img_dev * queries, itc), jnp.bfloat16),
            pltpu.VMEM((cap_dev * length, itc), jnp.bfloat16),
            pltpu.VMEM((n_img * n_cap, 8, cap_dev * length), jnp.float32),
            pltpu.VMEM((n_img, n_cap, cap_dev, slots), jnp.float32),
            pltpu.VMEM((slots, width), jnp.bfloat16),
            pltpu.VMEM((n_img * n_cap * cap_dev, embed_width), jnp.bfloat16),
            pltpu.SemaphoreType.DMA((10,)),
            pltpu.SemaphoreType.DMA((2 + CHUNKS, 4, 4)),
            pltpu.SemaphoreType.DMA((2 + CHUNKS, 4, 4)),
            pltpu.SemaphoreType.DMA((n_img * n_cap,)),
            pltpu.SemaphoreType.DMA((n_img * n_cap,)),
        ],
        compiler_params=pltpu.CompilerParams(
            collective_id=0, has_side_effects=True, vmem_limit_bytes=60 * 1024 * 1024
        ),
    )(*args)
    proj_grad = jnp.dot(feats, grads, preferred_element_type=jnp.float32)
    return (losses.reshape(cap_dev), proj_grad)


def solution(mesh):
    small = mesh.shape["img"] == 4 and mesh.shape["cap"] == 4
    local = fused if small else gathered
    in_specs = (
        P(("groups", "img", "cap"), None, None),
        P(("groups", "img", "cap")),
        P(),
        P(("groups", "img"), None, None),
        P(),
        P(("groups", "img", "cap"), None),
        P(("groups", "img"), None),
        P(),
        P(("groups", "img", "cap"), None),
    )
    out_specs = (P(("groups", "img", "cap")), P("groups", None))
    return jax.shard_map(local, mesh=mesh, in_specs=in_specs, out_specs=out_specs, check_vma=False)
```
